32 devices in a mesh: grp: 1, filt: 32 (over z, y, x, core).
Axes of the slice: x: 2, y: 2, z: 4, core: 2. Of those that a mesh axis runs over, the one named last changes fastest.
Arguments:
- code_maps: bfloat16 [256, 512, 512], P('filt', 'grp'), may hold values from -6 to 6
- dual_maps: bfloat16 [256, 512, 512], P('filt', 'grp'), may hold values from -4 to 4
- survey_tile: float32 [512, 512], P('grp'), may hold values from -192 to 192
- filters: float32 [256, 121], P('filt', 'grp'), may hold values from -6 to 6
- valid_blocks: int32 [4], P('grp'), may hold values from 0 to 1, as said below
Outputs:
- new_codes: bfloat16 [256, 512, 512], P('filt', 'grp')
- new_duals: bfloat16 [256, 512, 512], P('filt', 'grp')
- new_filters: float32 [256, 121], P('filt', 'grp')
The draws below stay inside these ranges and needn't reach their ends.
Inputs may be any that keep to these rules, and one draw needn't show every extreme that they name: `valid_blocks`: exactly 2 of the 4 blocks are 1, the others 0.
All inputs are finite; a program needn't handle non-finite values.
Results may differ from the reference program's by a relative error of at most 0.012.
The reference program's roundings to bfloat16 on the way count: a program that leaves them out, or rounds other values in their place, can miss the bound.
Values sent between devices are 32-bit elements; how exact they have to be, the bound alone decides.
A program may use at most 256 MiB of HBM per device.

```python
import math
import jax
import jax.numpy as jnp
from jax import lax

K = 256
N = 512
FS = 11
MB = 128
NB = 4


def draw_valid_blocks(key, part):
    key = jax.random.fold_in(key, 11)
    ordering = jax.random.permutation(key, NB)
    return (ordering < NB // 2).astype(jnp.int32)


def level_of(rng, shape, shards, smallest, top_value):
    level, own = 1.0, jax.random.fold_in(rng, 6)
    for dim, parts in shards:
        draws = jnp.exp(jax.random.uniform(jax.random.fold_in(own, dim), (parts,), jnp.float32, smallest / len(shards), top_value / len(shards)))
        level = level * jnp.repeat(draws, shape[dim] // parts).reshape([-1 if axis == dim else 1 for axis in range(len(shape))])
    return level


def bell_draw(own_key, extent, width, bound, cuts=(), held_as=jnp.bfloat16):
    factor_of = level_of(own_key, extent, cuts, -0.22, 0.18) if cuts else 1.0
    values = jax.random.normal(own_key, extent, jnp.float32) * width * factor_of
    return jnp.minimum(jnp.maximum(values, -bound), bound).astype(held_as)


def setup_inputs(seed: int = 0, part: int = 0) -> dict:
    splits = jax.random.split(jax.random.key(seed), 6)
    part_keys = jax.random.split(jax.random.fold_in(splits[5], part), 6)
    code_maps = bell_draw(part_keys[0], (K, N, N), 0.5, 6.0, ((0, 32),))
    dual_maps = bell_draw(part_keys[1], (K, N, N), 0.25, 4.0, ((0, 32),))
    survey_tile = bell_draw(part_keys[2], (N, N), 32.0, 192.0, (), jnp.float32)
    filters = bell_draw(part_keys[3], (K, FS * FS), 1.0, 6.0, ((0, 32),), jnp.float32)
    valid_blocks = draw_valid_blocks(jax.random.fold_in(jax.random.fold_in(splits[5], part), 71), part)
    return {"code_maps": code_maps, "dual_maps": dual_maps, "survey_tile": survey_tile, "filters": filters, "valid_blocks": valid_blocks}


penalty = 128.0
shrink_level = 1.0
dict_scale = 0.0625
norm_eps = 1e-06

def dft_tables(tile_side):
    indices = jnp.arange(tile_side, dtype=jnp.int32)
    phases = indices[:, None] * indices[None, :] % tile_side
    angles = phases.astype(jnp.float32) * (2.0 * math.pi / tile_side)
    return (jnp.cos(angles), jnp.sin(angles))

def forward_map(source, cos_sin, stacked):
    tile_side = source.shape[0]
    halves = jnp.dot(source, cos_sin, preferred_element_type=jnp.float32).astype(jnp.bfloat16)
    blocks = jnp.dot(stacked, halves, preferred_element_type=jnp.float32)
    real_part = blocks[:tile_side, :tile_side] - blocks[tile_side:, tile_side:]
    imag_part = -(blocks[:tile_side, tile_side:] + blocks[tile_side:, :tile_side])
    return (real_part, imag_part)

def inverse_map(real_part, imag_part, cos_sin, neg_table):
    tile_side = real_part.shape[0]
    stack_in = jnp.concatenate([real_part, imag_part], axis=0)
    blocks = jnp.dot(stack_in, cos_sin, preferred_element_type=jnp.float32)
    q_real = blocks[:tile_side, :tile_side] - blocks[tile_side:, tile_side:]
    q_imag = blocks[:tile_side, tile_side:] + blocks[tile_side:, :tile_side]
    merged = jnp.concatenate([q_real, q_imag], axis=0).astype(jnp.bfloat16)
    return jnp.dot(neg_table, merged, preferred_element_type=jnp.float32) / float(tile_side * tile_side)

def inverse_exact(real_part, imag_part, cos_sin_wide, neg_table):
    tile_side = real_part.shape[0]
    stack_in = jnp.concatenate([real_part, imag_part], axis=0)
    blocks = jnp.dot(stack_in, cos_sin_wide, precision=lax.Precision.HIGHEST, preferred_element_type=jnp.float32)
    q_real = blocks[:tile_side, :tile_side] - blocks[tile_side:, tile_side:]
    q_imag = blocks[:tile_side, tile_side:] + blocks[tile_side:, :tile_side]
    merged = jnp.concatenate([q_real, q_imag], axis=0).astype(jnp.bfloat16)
    return jnp.dot(neg_table, merged, preferred_element_type=jnp.float32) / float(tile_side * tile_side)

def filter_spectrum(kernel, cos_full, sin_full):
    highest = lax.Precision.HIGHEST
    cos_top = cos_full[:FS, :]
    sin_top = sin_full[:FS, :]
    cos_left = cos_full[:, :FS]
    sin_left = sin_full[:, :FS]
    part_re = jnp.dot(kernel, cos_top, precision=highest, preferred_element_type=jnp.float32)
    part_im = -jnp.dot(kernel, sin_top, precision=highest, preferred_element_type=jnp.float32)
    spec_re = jnp.dot(cos_left, part_re, precision=highest, preferred_element_type=jnp.float32) + jnp.dot(sin_left, part_im, precision=highest, preferred_element_type=jnp.float32)
    spec_im = jnp.dot(cos_left, part_im, precision=highest, preferred_element_type=jnp.float32) - jnp.dot(sin_left, part_re, precision=highest, preferred_element_type=jnp.float32)
    return (spec_re, spec_im)

def crop_filter(spec_re, spec_im, cos_full, sin_full):
    highest = lax.Precision.HIGHEST
    tile_side = spec_re.shape[0]
    cos_top = cos_full[:FS, :]
    sin_top = sin_full[:FS, :]
    cos_left = cos_full[:, :FS]
    sin_left = sin_full[:, :FS]
    vec_re = jnp.dot(spec_re, cos_left, precision=highest, preferred_element_type=jnp.float32) - jnp.dot(spec_im, sin_left, precision=highest, preferred_element_type=jnp.float32)
    vec_im = jnp.dot(spec_re, sin_left, precision=highest, preferred_element_type=jnp.float32) + jnp.dot(spec_im, cos_left, precision=highest, preferred_element_type=jnp.float32)
    raw_filter = (jnp.dot(cos_top, vec_re, precision=highest, preferred_element_type=jnp.float32) - jnp.dot(sin_top, vec_im, precision=highest, preferred_element_type=jnp.float32)) / float(tile_side * tile_side)
    rescale = lax.rsqrt(jnp.mean(raw_filter * raw_filter) + norm_eps)
    return (raw_filter * rescale).reshape(FS * FS)

def reference(code_maps, dual_maps, survey_tile, filters, valid_blocks):
    tile_side = survey_tile.shape[0]
    cos_full, sin_full = dft_tables(tile_side)
    cos_b = cos_full.astype(jnp.bfloat16)
    sin_b = sin_full.astype(jnp.bfloat16)
    cos_sin = jnp.concatenate([cos_b, sin_b], axis=1)
    cos_sin_wide = cos_sin.astype(jnp.float32)
    stacked = jnp.concatenate([cos_b, sin_b], axis=0)
    neg_table = jnp.concatenate([cos_b, -sin_b], axis=1)
    kernels = filters.reshape(K, FS, FS)
    zeros_map = jnp.zeros((tile_side, tile_side), jnp.float32)
    dict_weight = dict_scale * float(tile_side * tile_side)

    def first_pass(totals, pieces):
        kernel, code_map, dual_map = pieces
        d_re, d_im = filter_spectrum(kernel, cos_full, sin_full)
        z_re, z_im = forward_map(code_map, cos_sin, stacked)
        code_gap = (code_map.astype(jnp.float32) - dual_map.astype(jnp.float32)).astype(jnp.bfloat16)
        b_re, b_im = forward_map(code_gap, cos_sin, stacked)
        q_re, q_im, d_norm = totals
        totals = (q_re + d_re * z_re - d_im * z_im, q_im + d_re * z_im + d_im * z_re, d_norm + d_re * d_re + d_im * d_im)
        return (totals, jnp.stack([b_re, b_im]))
    (q_re, q_im, d_norm), gap_spectra = lax.scan(first_pass, (zeros_map, zeros_map, zeros_map), (kernels, code_maps, dual_maps))
    rebuilt = inverse_exact(q_re, q_im, cos_sin_wide, neg_table)
    row_mask = jnp.repeat(valid_blocks, MB).astype(jnp.float32)[:, None]
    filled = row_mask * survey_tile + (1.0 - row_mask) * rebuilt
    s_re, s_im = forward_map(filled.astype(jnp.bfloat16), cos_sin, stacked)

    def second_pass(totals, pieces):
        kernel, gap_pair = pieces
        d_re, d_im = filter_spectrum(kernel, cos_full, sin_full)
        b_re = d_re * s_re + d_im * s_im + penalty * gap_pair[0]
        b_im = d_re * s_im - d_im * s_re + penalty * gap_pair[1]
        e_re, e_im = totals
        return ((e_re + d_re * b_re - d_im * b_im, e_im + d_re * b_im + d_im * b_re), jnp.stack([b_re, b_im]))
    (e_re, e_im), rhs_spectra = lax.scan(second_pass, (zeros_map, zeros_map), (kernels, gap_spectra))
    divisor = penalty + d_norm
    t_re = e_re / divisor
    t_im = e_im / divisor

    def third_pass(totals, pieces):
        kernel, rhs_pair, dual_map = pieces
        d_re, d_im = filter_spectrum(kernel, cos_full, sin_full)
        x_re = (rhs_pair[0] - (d_re * t_re + d_im * t_im)) / penalty
        x_im = (rhs_pair[1] - (d_re * t_im - d_im * t_re)) / penalty
        spatial = inverse_map(x_re.astype(jnp.bfloat16), x_im.astype(jnp.bfloat16), cos_sin, neg_table)
        shifted = spatial + dual_map.astype(jnp.float32)
        shrunk = jnp.sign(shifted) * jnp.maximum(jnp.abs(shifted) - shrink_level, 0.0)
        c_re = x_re * s_re + x_im * s_im + dict_weight * d_re
        c_im = x_re * s_im - x_im * s_re + dict_weight * d_im
        own_den = dict_weight + x_re * x_re + x_im * x_im
        new_filter = crop_filter(c_re / own_den, c_im / own_den, cos_full, sin_full)
        return (totals, (shrunk.astype(jnp.bfloat16), (shifted - shrunk).astype(jnp.bfloat16), new_filter))
    unused, (new_codes, new_duals, new_filters) = lax.scan(third_pass, jnp.zeros((), jnp.float32), (kernels, rhs_spectra, dual_maps))
    return (new_codes, new_duals, new_filters)
```

```python
import math

import jax
import jax.numpy as jnp
import ml_dtypes
import numpy as np
from jax import lax
from jax.experimental import pallas as pl
from jax.experimental.pallas import tpu as pltpu
from jax.sharding import PartitionSpec as P

FS = 11
MB = 128
PAD = 16
TERMS = 6
TAPS = 32
SUB = 8
LANES = 128

penalty = 128.0
shrink_level = 1.0
dict_scale = 0.0625
norm_eps = 1e-06

VMEM_LIMIT = 60 * 1024 * 1024
BF = ml_dtypes.bfloat16


def split_np(a, parts):
    out, rest = [], np.asarray(a, np.float32)
    for _ in range(parts):
        piece = rest.astype(BF)
        out.append(piece)
        rest = rest - piece.astype(np.float32)
    return out


def make_tables(n):
    half = n // 2
    hr = half + PAD
    idx = np.arange(n)
    phases = (idx[:, None] * idx[None, :]) % n
    angles = phases.astype(np.float32) * np.float32(2.0 * math.pi / n)
    c, s = np.cos(angles).astype(np.float32), np.sin(angles).astype(np.float32)
    cb, sb = c.astype(BF), s.astype(BF)
    perm = np.concatenate([np.arange(half), [half], n - np.arange(1, half)])
    weight = np.full((half + 1,), 2.0, np.float32)
    weight[0] = weight[half] = 1.0

    s_pack = sb[:, :half].copy()
    s_pack[:, 0] = cb[:, half]
    first = np.concatenate([cb[:, :half], s_pack], axis=1)

    second = np.zeros((2 * hr, n), BF)
    second[: half + 1] = cb[: half + 1]
    second[hr : hr + half + 1] = sb[: half + 1]

    inv_first = np.concatenate([cb[perm], sb[perm]], axis=1)

    wf = weight[:half][None, :]
    ti_c = cb[:, :half].astype(np.float32) * wf
    ti_s = -sb[:, :half].astype(np.float32) * wf
    ti_s[:, 0] = cb[:, half].astype(np.float32)
    inv_second = (np.concatenate([ti_c, ti_s], axis=1) / float(n * n)).astype(BF)

    left = np.zeros((2 * hr, 2 * PAD), np.float32)
    left[: half + 1, :FS] = c[: half + 1, :FS]
    left[: half + 1, PAD : PAD + FS] = s[: half + 1, :FS]
    left[hr : hr + half + 1, :FS] = -s[: half + 1, :FS]
    left[hr : hr + half + 1, PAD : PAD + FS] = c[: half + 1, :FS]
    l0, l1, l2 = split_np(left, 3)
    left6 = np.concatenate([l0, l0, l1, l0, l1, l2], axis=1)
    top = np.concatenate([c[:FS][:, perm], -s[:FS][:, perm]], axis=1)

    crop = np.zeros((n, 128), BF)
    for at, table in ((0, c), (PAD, s)):
        hi, lo = split_np(table[perm][:, :FS], 2)
        crop[:, at : at + FS] = hi
        crop[:, 2 * PAD + at : 2 * PAD + at + FS] = lo
    rows = np.zeros((2 * PAD, 2 * hr), np.float32)
    wc = c[:FS, : half + 1] * weight[None, :]
    ws = s[:FS, : half + 1] * weight[None, :]
    rows[:FS, : half + 1] = wc
    rows[:FS, hr : hr + half + 1] = -ws
    rows[PAD : PAD + FS, : half + 1] = -ws
    rows[PAD : PAD + FS, hr : hr + half + 1] = -wc
    r_hi, r_lo = split_np(rows, 2)
    crop_rows = np.concatenate([r_hi, r_lo], axis=0)

    grid = np.arange(TAPS)
    turn = 2.0 * math.pi / TAPS
    a_of, b_of = np.divmod(np.arange(FS * FS), FS)
    ang = turn * ((a_of[:, None] * np.repeat(grid, TAPS)[None, :] + b_of[:, None] * np.tile(grid, TAPS)[None, :]) % TAPS)
    sample = np.concatenate([np.cos(ang), np.sin(ang)], axis=1).astype(np.float32)
    taps = np.arange(-(FS - 1), FS)

    def interp(freqs):
        diff = freqs[:, None] * (2.0 * math.pi / n) - grid[None, :] * turn
        return np.cos(diff[:, :, None] * taps[None, None, :]).sum(axis=2) / TAPS

    up_rows = np.zeros((hr, TAPS), np.float32)
    up_rows[: half + 1] = interp(np.arange(half + 1))
    up_cols = np.zeros((LANES, n), np.float32)
    up_cols[:TAPS] = interp(perm).T
    return dict(
        sample=sample, up_rows=up_rows, up_cols=up_cols,
        first=first, second=second, inv_first=inv_first, inv_second=inv_second,
        left6=left6, top=top, crop=crop, crop_rows=crop_rows,
    )


def mm(a, b):
    return jnp.dot(a, b, preferred_element_type=jnp.float32)


def spectrum_rows(y_ref, hr, half, r0, rb):
    rows, srows = pl.ds(r0, rb), pl.ds(hr + r0, rb)
    cc, cs = y_ref[rows, :half], y_ref[rows, half:]
    sc, ss = y_ref[srows, :half], y_ref[srows, half:]
    col0 = lax.broadcasted_iota(jnp.int32, (rb, half), 1) == 0
    zero = jnp.zeros_like(cc)
    plus = (cc - jnp.where(col0, zero, ss), -(sc + jnp.where(col0, zero, cs)))
    minus = (jnp.where(col0, cs, cc + ss), jnp.where(col0, -ss, cs - sc))
    return plus, minus


def sums_kernel(n, code_ref, dual_ref, td_ref, energy_ref, first_ref, second_ref, left_ref, acc_ref, b_ref, p_ref, yz_ref, yb_ref, d_ref):
    half = n // 2
    hr = half + PAD

    @pl.when(pl.program_id(0) == 0)
    def _():
        acc_ref[...] = jnp.zeros_like(acc_ref)

    code = code_ref[0]
    gap = (code.astype(jnp.float32) - dual_ref[0].astype(jnp.float32)).astype(jnp.bfloat16)
    d_ref[...] = mm(left_ref[...], td_ref[0])
    p_ref[0] = mm(code, first_ref[...]).astype(jnp.bfloat16)
    p_ref[1] = mm(gap, first_ref[...]).astype(jnp.bfloat16)
    yz_ref[...] = mm(second_ref[...], p_ref[0])
    yb_ref[...] = mm(second_ref[...], p_ref[1])
    rb = 2 * SUB
    for r0 in range(0, hr, rb):
        rows, srows = pl.ds(r0, rb), pl.ds(hr + r0, rb)
        z_halves = spectrum_rows(yz_ref, hr, half, r0, rb)
        b_halves = spectrum_rows(yb_ref, hr, half, r0, rb)
        for h in range(2):
            cols = slice(h * half, (h + 1) * half)
            d_re, d_im = d_ref[rows, cols], d_ref[srows, cols]
            z_re, z_im = z_halves[h]
            b_re, b_im = b_halves[h]
            b_ref[0, 0, rows, cols] = b_re
            b_ref[0, 1, rows, cols] = b_im
            terms = (
                d_re * z_re - d_im * z_im, d_re * z_im + d_im * z_re,
                d_re * b_re - d_im * b_im, d_re * b_im + d_im * b_re,
            )
            for part, term in enumerate(terms):
                for c in range(half // LANES):
                    at = tile_at(n, part, h * (half // LANES) + c, r0)
                    acc_ref[pl.ds(at, 2)] += term[:, c * LANES : (c + 1) * LANES].reshape(2, SUB, LANES)

    @pl.when(pl.program_id(0) == pl.num_programs(0) - 1)
    def _():
        for c in range(TAPS // SUB):
            acc_ref[tile_at(n, 0, c, hr - SUB)] = energy_ref[c]


def tile_at(n, part, group, row):
    return (part * (n // LANES) + group) * ((n // 2 + PAD) // SUB) + row // SUB


def load_rows(ref, n, part, r0, rb, first, last):
    pieces = [ref[pl.ds(tile_at(n, part, g, r0), rb // SUB)].reshape(rb, LANES) for g in range(first, last)]
    return jnp.concatenate(pieces, axis=1)


def sum_stages(devices):
    bits = devices.bit_length() - 1
    if devices != 1 << bits:
        raise ValueError("bad count")
    low = (bits - 1) // 2
    sizes = [1, low, bits - 1 - low] if bits else []
    stages, stride = [], 1
    for size in sizes:
        if size > 0:
            stages.append((1 << size, stride))
        stride <<= max(size, 0)
    return stages


def exchange_kernel(stages, lanes, x_ref, out_ref, sum_ref, recv_ref, rs_send, rs_recv, ag_send, ag_recv):
    me = lax.axis_index("filt")
    digits = [lax.rem(me // stride, radix) for radix, stride in stages]

    def peer_of(stage, digit):
        return me + (digit - digits[stage]) * stages[stage][1]

    barrier = pltpu.get_barrier_semaphore()
    count = 0
    for stage, (radix, _) in enumerate(stages):
        for d in range(1, radix):
            pl.semaphore_signal(
                barrier, inc=1, device_id={"filt": peer_of(stage, lax.rem(digits[stage] + d, radix))},
                device_id_type=pl.DeviceIdType.MESH,
            )
            count += 1
    pl.semaphore_wait(barrier, count)

    plans = []
    slot, sem = 0, 0
    for start, total, order in lanes:
        base, size, plan = start, total, []
        for position, stage in enumerate(order):
            radix = stages[stage][0]
            sub = size // radix
            plan.append((position, stage, radix, base, sub, slot, sem))
            base = base + digits[stage] * sub
            size = sub
            slot += (radix - 1) * sub
            sem += radix - 1
        plans.append(plan)

    def scatter(entry):
        position, stage, radix, base, sub, slot, sem = entry
        source = x_ref if position == 0 else sum_ref
        copies = []
        for d in range(1, radix):
            target = lax.rem(digits[stage] + d, radix)
            copies.append(pltpu.make_async_remote_copy(
                src_ref=source.at[pl.ds(base + target * sub, sub)],
                dst_ref=recv_ref.at[pl.ds(slot + (d - 1) * sub, sub)],
                send_sem=rs_send.at[sem + d - 1], recv_sem=rs_recv.at[sem + d - 1],
                device_id={"filt": peer_of(stage, target)}, device_id_type=pl.DeviceIdType.MESH,
            ))
        return copies

    def add_up(entry):
        position, stage, radix, base, sub, slot, sem = entry
        source = x_ref if position == 0 else sum_ref
        own = base + digits[stage] * sub
        result = out_ref if position == len(stages) - 1 else sum_ref
        step = max(w for w in range(1, 17) if sub % w == 0)

        def add(i, carry):
            value = source[pl.ds(own + i * step, step)]
            for d in range(1, radix):
                value = value + recv_ref[pl.ds(slot + (d - 1) * sub + i * step, step)]
            result[pl.ds(own + i * step, step)] = value
            return carry

        lax.fori_loop(0, sub // step, add, 0)

    def gather(entry):
        position, stage, radix, base, sub, slot, sem = entry
        own = pl.ds(base + digits[stage] * sub, sub)
        copies = []
        for d in range(1, radix):
            target = lax.rem(digits[stage] + d, radix)
            copies.append(pltpu.make_async_remote_copy(
                src_ref=out_ref.at[own], dst_ref=out_ref.at[own],
                send_sem=ag_send.at[sem + d - 1], recv_sem=ag_recv.at[sem + d - 1],
                device_id={"filt": peer_of(stage, target)}, device_id_type=pl.DeviceIdType.MESH,
            ))
        return copies

    depth = len(stages)
    flight = [None] * len(lanes)
    for step in range(2 * depth + 1):
        for lane in range(len(lanes)):
            if flight[lane] is not None:
                for copy in flight[lane]:
                    copy.wait()
                if step <= depth:
                    add_up(plans[lane][step - 1])
            if step < 2 * depth:
                entry = plans[lane][step if step < depth else 2 * depth - 1 - step]
                flight[lane] = scatter(entry) if step < depth else gather(entry)
                for copy in flight[lane]:
                    copy.start()


def fold_first(blk_ref, q_ref, n):
    half = n // 2
    hr = half + PAD
    rb = 16
    for r0 in range(0, half, rb):
        rows, srows = pl.ds(r0, rb), pl.ds(hr + r0, rb)
        q_re = blk_ref[rows, :n] - blk_ref[srows, n:]
        q_im = blk_ref[rows, n:] + blk_ref[srows, :n]
        if r0 == 0:
            last = blk_ref[half : half + 8, :n] - blk_ref[hr + half : hr + half + 8, n:]
            row0 = lax.broadcasted_iota(jnp.int32, (rb, n), 0) == 0
            q_im = jnp.where(row0, jnp.broadcast_to(last[0:1], (rb, n)), q_im)
        q_ref[rows, :] = q_re.astype(jnp.bfloat16)
        q_ref[pl.ds(half + r0, rb), :] = q_im.astype(jnp.bfloat16)


def update_kernel(
    n, sums_ref, up_rows_ref, up_cols_ref, survey_ref, mask_ref, b_ref, dual_ref, td_ref, first_ref, second_ref, inv_first_ref,
    inv_second_ref, left_ref, crop_ref, crop_rows_ref,
    codes_ref, duals_ref, raw_ref,
    s_ref, r_ref, d_ref, x_ref, e_ref, blk_ref, q_ref,
):
    half = n // 2
    hr = half + PAD
    rb = 16
    dict_weight = dict_scale * float(n * n)

    @pl.when(pl.program_id(0) == 0)
    def _():
        for r0 in range(0, hr, rb):
            rows, srows = pl.ds(r0, rb), pl.ds(hr + r0, rb)
            for part, at in ((0, rows), (1, srows)):
                v = load_rows(sums_ref, n, part, r0, rb, 0, n // LANES)
                hi = v.astype(jnp.bfloat16)
                rest = v - hi.astype(jnp.float32)
                mid = rest.astype(jnp.bfloat16)
                x_ref[at, :] = hi
                e_ref[pl.ds(part * hr + r0, rb), :] = mid
                e_ref[pl.ds((2 + part) * hr + r0, rb), :] = (rest - mid.astype(jnp.float32)).astype(jnp.bfloat16)
        blk_ref[...] = mm(x_ref[...], inv_first_ref[...])
        blk_ref[...] += mm(e_ref[: 2 * hr, :], inv_first_ref[...])
        blk_ref[...] += mm(e_ref[2 * hr :, :], inv_first_ref[...])
        fold_first(blk_ref, q_ref, n)
        rebuilt = mm(inv_second_ref[...], q_ref[...])
        m = mask_ref[...]
        filled = (m * survey_ref[...] + (1.0 - m) * rebuilt).astype(jnp.bfloat16)
        q_ref[...] = mm(filled, first_ref[...]).astype(jnp.bfloat16)
        d_ref[...] = mm(second_ref[...], q_ref[...])
        samples = jnp.concatenate([sums_ref[tile_at(n, 0, c, hr - SUB)] for c in range(TAPS // SUB)], axis=0)
        exact = dict(precision=lax.Precision.HIGHEST, preferred_element_type=jnp.float32)
        r_ref[0] = jnp.dot(jnp.dot(up_rows_ref[...], samples, **exact), up_cols_ref[...], **exact)
        for r0 in range(0, hr, rb):
            rows = pl.ds(r0, rb)
            halves = spectrum_rows(d_ref, hr, half, r0, rb)
            for h in range(2):
                cols = slice(h * half, (h + 1) * half)
                s_re, s_im = halves[h]
                scale = 1.0 / (penalty + jnp.maximum(r_ref[0, rows, cols], 0.0))
                g0, g1 = h * (half // LANES), (h + 1) * (half // LANES)
                s_ref[0, rows, cols] = s_re
                s_ref[1, rows, cols] = s_im
                r_ref[0, rows, cols] = (s_re - load_rows(sums_ref, n, 2, r0, rb, g0, g1)) * scale
                r_ref[1, rows, cols] = (s_im - load_rows(sums_ref, n, 3, r0, rb, g0, g1)) * scale

    d_ref[...] = mm(left_ref[...], td_ref[0])
    for r0 in range(0, hr, rb):
        rows, srows = pl.ds(r0, rb), pl.ds(hr + r0, rb)
        for h in range(2):
            cols = slice(h * half, (h + 1) * half)
            d_re, d_im = d_ref[rows, cols], d_ref[srows, cols]
            r_re, r_im = r_ref[0, rows, cols], r_ref[1, rows, cols]
            s_re, s_im = s_ref[0, rows, cols], s_ref[1, rows, cols]
            x_re = b_ref[0, 0, rows, cols] + (d_re * r_re + d_im * r_im)
            x_im = b_ref[0, 1, rows, cols] + (d_re * r_im - d_im * r_re)
            x_ref[rows, cols] = x_re.astype(jnp.bfloat16)
            x_ref[srows, cols] = x_im.astype(jnp.bfloat16)
            inv = 1.0 / (dict_weight + x_re * x_re + x_im * x_im)
            e_re = (x_re * s_re + x_im * s_im + dict_weight * d_re) * inv
            e_im = (x_re * s_im - x_im * s_re + dict_weight * d_im) * inv
            for part, e in ((0, e_re), (1, e_im)):
                hi = e.astype(jnp.bfloat16)
                e_ref[pl.ds(part * hr + r0, rb), cols] = hi
                e_ref[pl.ds((2 + part) * hr + r0, rb), cols] = (e - hi.astype(jnp.float32)).astype(jnp.bfloat16)
    blk_ref[...] = mm(x_ref[...], inv_first_ref[...])
    v = mm(e_ref[: 2 * hr, :], crop_ref[...]) + mm(e_ref[2 * hr :, :], crop_ref[...])
    v_hi = v.astype(jnp.bfloat16)
    v_lo = (v - v_hi.astype(jnp.float32)).astype(jnp.bfloat16)
    raw_ref[0] = mm(crop_rows_ref[...], v_hi) + mm(crop_rows_ref[...], v_lo)
    fold_first(blk_ref, q_ref, n)
    shifted = mm(inv_second_ref[...], q_ref[...]) + dual_ref[0].astype(jnp.float32)
    shrunk = shifted - jnp.clip(shifted, -shrink_level, shrink_level)
    codes_ref[0] = shrunk.astype(jnp.bfloat16)
    duals_ref[0] = (shifted - shrunk).astype(jnp.bfloat16)


def whole_spec(shape):
    return pl.BlockSpec(shape, lambda k: (0,) * len(shape))


def per_filter(shape):
    return pl.BlockSpec((1,) + shape, lambda k: (k,) + (0,) * len(shape))


def filter_terms(filters, top, n):
    count = filters.shape[0]
    kernels = filters.reshape(count, FS, FS)
    t = jnp.einsum("kab,bg->kag", kernels, top, precision=lax.Precision.HIGHEST, preferred_element_type=jnp.float32)
    gap = ((0, 0), (0, PAD - FS), (0, 0))
    t = jnp.concatenate([jnp.pad(t[:, :, :n], gap), jnp.pad(t[:, :, n:], gap)], axis=1)
    t0 = t.astype(jnp.bfloat16)
    rest = t - t0.astype(jnp.float32)
    t1 = rest.astype(jnp.bfloat16)
    t2 = (rest - t1.astype(jnp.float32)).astype(jnp.bfloat16)
    return jnp.concatenate([t0, t1, t0, t2, t1, t0], axis=1)


def energy_samples(filters, sample):
    spec = jnp.dot(filters, sample, precision=lax.Precision.HIGHEST, preferred_element_type=jnp.float32)
    energy = jnp.sum(spec * spec, axis=0).reshape(2, TAPS, TAPS).sum(axis=0)
    return jnp.pad(energy, ((0, 0), (0, LANES - TAPS))).reshape(TAPS // SUB, SUB, LANES)


def sum_plan(mesh, tiles):
    devices = mesh.shape["filt"]
    stages = sum_stages(devices)
    units = -(-tiles // devices)
    order = list(range(len(stages)))
    if len(stages) == 3 and units >= 4:
        other = max(1, (units * 4) // 17)
        rest = units - other
        sizes = [(rest + 2) // 3, other, (rest + 1) // 3, rest // 3]
        orders = [order, [0, 2, 1], order, order]
    else:
        sizes, orders = [units], [order]
    lanes, start = [], 0
    for size, own in zip(sizes, orders):
        lanes.append((start, size * devices, own))
        start += size * devices
    return stages, lanes, start


def reduce_tiles(acc, stages, lanes):
    if not stages:
        return acc
    room = 0
    for _, size, order in lanes:
        for stage in order:
            radix = stages[stage][0]
            size //= radix
            room += (radix - 1) * size
    sems = len(lanes) * sum(radix - 1 for radix, _ in stages)
    return pl.pallas_call(
        lambda *refs: exchange_kernel(stages, lanes, *refs),
        out_shape=jax.ShapeDtypeStruct(acc.shape, acc.dtype),
        in_specs=[pl.BlockSpec(memory_space=pltpu.VMEM)],
        out_specs=pl.BlockSpec(memory_space=pltpu.VMEM),
        scratch_shapes=[pltpu.VMEM(acc.shape, jnp.float32), pltpu.VMEM((room, SUB, LANES), jnp.float32)] + [pltpu.SemaphoreType.DMA((sems,))] * 4,
        compiler_params=pltpu.CompilerParams(collective_id=0, has_side_effects=True, vmem_limit_bytes=VMEM_LIMIT),
        name="exchange",
    )(acc)


def make_body(mesh):
    def body(code_maps, dual_maps, survey_tile, filters, valid_blocks):
        n = survey_tile.shape[0]
        count = code_maps.shape[0]
        hr = n // 2 + PAD
        t = make_tables(n)
        td = filter_terms(filters, t["top"], n)
        kdim = td.shape[1]
        f32, bf16 = jnp.float32, jnp.bfloat16
        params = pltpu.CompilerParams(vmem_limit_bytes=VMEM_LIMIT, dimension_semantics=("arbitrary",))
        stages, lanes, tiles = sum_plan(mesh, 4 * (n // LANES) * (hr // SUB))
        energy = energy_samples(filters, t["sample"])
        acc, b = pl.pallas_call(
            lambda *refs: sums_kernel(n, *refs),
            grid=(count,),
            in_specs=[per_filter((n, n)), per_filter((n, n)), per_filter((kdim, n)),
                      whole_spec((TAPS // SUB, SUB, LANES)), whole_spec((n, n)), whole_spec((2 * hr, n)), whole_spec((2 * hr, kdim))],
            out_specs=[whole_spec((tiles, SUB, LANES)), per_filter((2, hr, n))],
            out_shape=[jax.ShapeDtypeStruct((tiles, SUB, LANES), f32), jax.ShapeDtypeStruct((count, 2, hr, n), f32)],
            scratch_shapes=[pltpu.VMEM((2, n, n), bf16)] + [pltpu.VMEM((2 * hr, n), f32)] * 3,
            compiler_params=params,
            name="sums",
        )(code_maps, dual_maps, td, energy, t["first"], t["second"], t["left6"])
        sums = reduce_tiles(acc, stages, lanes)
        mask = jnp.repeat(valid_blocks, MB).astype(f32)[:, None]
        new_codes, new_duals, crops = pl.pallas_call(
            lambda *refs: update_kernel(n, *refs),
            grid=(count,),
            in_specs=[whole_spec((tiles, SUB, LANES)), whole_spec((hr, TAPS)), whole_spec((LANES, n)), whole_spec((n, n)), whole_spec((n, 1)), per_filter((2, hr, n)),
                      per_filter((n, n)), per_filter((kdim, n)), whole_spec((n, n)), whole_spec((2 * hr, n)),
                      whole_spec((n, 2 * n)), whole_spec((n, n)), whole_spec((2 * hr, kdim)),
                      whole_spec((n, 128)), whole_spec((4 * PAD, 2 * hr))],
            out_specs=[per_filter((n, n)), per_filter((n, n)), per_filter((4 * PAD, 128))],
            out_shape=[jax.ShapeDtypeStruct((count, n, n), bf16), jax.ShapeDtypeStruct((count, n, n), bf16),
                       jax.ShapeDtypeStruct((count, 4 * PAD, 128), f32)],
            scratch_shapes=[pltpu.VMEM((2, hr, n), f32), pltpu.VMEM((2, hr, n), f32), pltpu.VMEM((2 * hr, n), f32),
                            pltpu.VMEM((2 * hr, n), bf16), pltpu.VMEM((4 * hr, n), bf16),
                            pltpu.VMEM((2 * hr, 2 * n), f32), pltpu.VMEM((n, n), bf16)],
            compiler_params=params,
            name="update",
        )(sums, t["up_rows"], t["up_cols"], survey_tile, mask, b, dual_maps, td, t["first"], t["second"], t["inv_first"],
          t["inv_second"], t["left6"], t["crop"], t["crop_rows"])
        m = crops[:, : 2 * PAD] + crops[:, 2 * PAD :]
        m = m[:, :, : 2 * PAD] + m[:, :, 2 * PAD : 4 * PAD]
        raw = (m[:, :FS, :FS] + m[:, PAD : PAD + FS, PAD : PAD + FS]) / float(n * n)
        rescale = lax.rsqrt(jnp.mean(raw * raw, axis=(1, 2), keepdims=True) + norm_eps)
        return new_codes, new_duals, (raw * rescale).reshape(count, FS * FS)

    return body


def solution(mesh):
    return jax.shard_map(
        make_body(mesh),
        mesh=mesh,
        in_specs=(
            P("filt", "grp", None),
            P("filt", "grp", None),
            P("grp", None),
            P("filt", "grp"),
            P("grp"),
        ),
        out_specs=(P("filt", "grp", None), P("filt", "grp", None), P("filt", "grp")),
        check_vma=False,
    )
```

```python
import math

import jax
import jax.numpy as jnp
import ml_dtypes
import numpy as np
from jax import lax
from jax.experimental import pallas as pl
from jax.experimental.pallas import tpu as pltpu
from jax.sharding import PartitionSpec as P

FS = 11
MB = 128
PAD = 16
TERMS = 6
TAPS = 32
SUB = 8
SUM_FILTERS = 1
UPDATE_FILTERS = 2
LANES = 128

penalty = 128.0
shrink_level = 1.0
dict_scale = 0.0625
norm_eps = 1e-06

VMEM_LIMIT = 60 * 1024 * 1024
BF = ml_dtypes.bfloat16


def split_np(a, parts):
    out, rest = [], np.asarray(a, np.float32)
    for _ in range(parts):
        piece = rest.astype(BF)
        out.append(piece)
        rest = rest - piece.astype(np.float32)
    return out


def make_tables(n):
    half = n // 2
    hr = half + PAD
    idx = np.arange(n)
    phases = (idx[:, None] * idx[None, :]) % n
    angles = phases.astype(np.float32) * np.float32(2.0 * math.pi / n)
    c, s = np.cos(angles).astype(np.float32), np.sin(angles).astype(np.float32)
    cb, sb = c.astype(BF), s.astype(BF)
    perm = np.concatenate([np.arange(half), [half], n - np.arange(1, half)])
    weight = np.full((half + 1,), 2.0, np.float32)
    weight[0] = weight[half] = 1.0

    s_pack = sb[:, :half].copy()
    s_pack[:, 0] = cb[:, half]
    first = np.concatenate([cb[:, :half], s_pack], axis=1)

    second = np.zeros((2 * hr, n), BF)
    second[: half + 1] = cb[: half + 1]
    second[hr : hr + half + 1] = sb[: half + 1]

    inv_first = np.concatenate([cb[perm], sb[perm]], axis=1)

    wf = weight[:half][None, :]
    ti_c = cb[:, :half].astype(np.float32) * wf
    ti_s = -sb[:, :half].astype(np.float32) * wf
    ti_s[:, 0] = cb[:, half].astype(np.float32)
    inv_second = (np.concatenate([ti_c, ti_s], axis=1) / float(n * n)).astype(BF)

    left = np.zeros((2 * hr, 2 * PAD), np.float32)
    left[: half + 1, :FS] = c[: half + 1, :FS]
    left[: half + 1, PAD : PAD + FS] = s[: half + 1, :FS]
    left[hr : hr + half + 1, :FS] = -s[: half + 1, :FS]
    left[hr : hr + half + 1, PAD : PAD + FS] = c[: half + 1, :FS]
    l0, l1, l2 = split_np(left, 3)
    left6 = np.concatenate([l0, l0, l1, l0, l1, l2], axis=1)
    top = np.concatenate([c[:FS][:, perm], -s[:FS][:, perm]], axis=1)

    crop = np.zeros((n, 128), BF)
    for at, table in ((0, c), (PAD, s)):
        hi, lo = split_np(table[perm][:, :FS], 2)
        crop[:, at : at + FS] = hi
        crop[:, 2 * PAD + at : 2 * PAD + at + FS] = lo
    rows = np.zeros((2 * PAD, 2 * hr), np.float32)
    wc = c[:FS, : half + 1] * weight[None, :]
    ws = s[:FS, : half + 1] * weight[None, :]
    rows[:FS, : half + 1] = wc
    rows[:FS, hr : hr + half + 1] = -ws
    rows[PAD : PAD + FS, : half + 1] = -ws
    rows[PAD : PAD + FS, hr : hr + half + 1] = -wc
    r_hi, r_lo = split_np(rows, 2)
    crop_rows = np.concatenate([r_hi, r_lo], axis=0)

    grid = np.arange(TAPS)
    turn = 2.0 * math.pi / TAPS
    a_of, b_of = np.divmod(np.arange(FS * FS), FS)
    ang = turn * ((a_of[:, None] * np.repeat(grid, TAPS)[None, :] + b_of[:, None] * np.tile(grid, TAPS)[None, :]) % TAPS)
    sample = np.concatenate([np.cos(ang), np.sin(ang)], axis=1).astype(np.float32)
    taps = np.arange(-(FS - 1), FS)

    def interp(freqs):
        diff = freqs[:, None] * (2.0 * math.pi / n) - grid[None, :] * turn
        return np.cos(diff[:, :, None] * taps[None, None, :]).sum(axis=2) / TAPS

    up_rows = np.zeros((hr, TAPS), np.float32)
    up_rows[: half + 1] = interp(np.arange(half + 1))
    up_cols = np.zeros((LANES, n), np.float32)
    up_cols[:TAPS] = interp(perm).T
    return dict(
        sample=sample, up_rows=up_rows, up_cols=up_cols,
        first=first, second=second, inv_first=inv_first, inv_second=inv_second,
        left6=left6, top=top, crop=crop, crop_rows=crop_rows,
    )


def mm(a, b):
    return jnp.dot(a, b, preferred_element_type=jnp.float32)


def spectrum_rows(y_ref, hr, half, r0, rb):
    rows, srows = pl.ds(r0, rb), pl.ds(hr + r0, rb)
    cc, cs = y_ref[rows, :half], y_ref[rows, half:]
    sc, ss = y_ref[srows, :half], y_ref[srows, half:]
    col0 = lax.broadcasted_iota(jnp.int32, (rb, half), 1) == 0
    zero = jnp.zeros_like(cc)
    plus = (cc - jnp.where(col0, zero, ss), -(sc + jnp.where(col0, zero, cs)))
    minus = (jnp.where(col0, cs, cc + ss), jnp.where(col0, -ss, cs - sc))
    return plus, minus


def missing_blocks(valid_ref):
    first = jnp.where(valid_ref[0] == 0, 0, jnp.where(valid_ref[1] == 0, 1, 2))
    last = jnp.where(valid_ref[3] == 0, 3, jnp.where(valid_ref[2] == 0, 2, 1))
    return [pl.ds(pl.multiple_of(at * MB, MB), MB) for at in (first, last)]


def sums_kernel(
    n, valid_ref, code_ref, dual_ref, td_ref, energy_ref, first_ref, second_ref, left_ref, inv_first_ref, inv_second_ref,
    acc_ref, b_ref, p_ref, yz_ref, yb_ref, d_ref, q_ref, terms_ref, blk_ref, fold_ref,
):
    half = n // 2
    hr = half + PAD

    @pl.when(pl.program_id(0) == 0)
    def _():
        acc_ref[...] = jnp.zeros_like(acc_ref)
        q_ref[...] = jnp.zeros_like(q_ref)

    per = code_ref.shape[0]
    rb = 2 * SUB

    def first_sections(j):
        code = code_ref[j]
        gap = (code.astype(jnp.float32) - dual_ref[j].astype(jnp.float32)).astype(jnp.bfloat16)
        p_ref[j, 0] = mm(code, first_ref[...]).astype(jnp.bfloat16)
        p_ref[j, 1] = mm(gap, first_ref[...]).astype(jnp.bfloat16)

    def second_sections(j):
        d_ref[j] = mm(left_ref[...], td_ref[j])
        yz_ref[j] = mm(second_ref[...], p_ref[j, 0])
        yb_ref[j] = mm(second_ref[...], p_ref[j, 1])

    def add_products(j):
        for r0 in range(0, hr, rb):
            rows, srows = pl.ds(r0, rb), pl.ds(hr + r0, rb)
            z_halves = spectrum_rows(yz_ref.at[j], hr, half, r0, rb)
            b_halves = spectrum_rows(yb_ref.at[j], hr, half, r0, rb)
            for h in range(2):
                cols = slice(h * half, (h + 1) * half)
                d_re, d_im = d_ref[j, rows, cols], d_ref[j, srows, cols]
                z_re, z_im = z_halves[h]
                b_re, b_im = b_halves[h]
                b_ref[j, 0, rows, cols] = b_re
                b_ref[j, 1, rows, cols] = b_im
                q_ref[0, rows, cols] += d_re * z_re - d_im * z_im
                q_ref[1, rows, cols] += d_re * z_im + d_im * z_re
                for part, term in enumerate((d_re * b_re - d_im * b_im, d_re * b_im + d_im * b_re)):
                    for c in range(half // LANES):
                        at = tile_at(n, part, h * (half // LANES) + c, r0)
                        acc_ref[pl.ds(at, 2)] += term[:, c * LANES : (c + 1) * LANES].reshape(2, SUB, LANES)

    first_sections(0)
    for j in range(per):
        second_sections(j)
        if j + 1 < per:
            first_sections(j + 1)
        if j > 0:
            add_products(j - 1)
    add_products(per - 1)

    @pl.when(pl.program_id(0) == pl.num_programs(0) - 1)
    def _():
        for c in range(TAPS // SUB):
            acc_ref[tile_at(n, 0, c, hr - SUB)] = energy_ref[c]
        for r0 in range(0, hr, rb):
            for part in range(2):
                v = q_ref[part, pl.ds(r0, rb), :]
                at = pl.ds(part * hr + r0, rb)
                for term in range(3):
                    piece = v.astype(jnp.bfloat16)
                    terms_ref[term, at, :] = piece
                    v = v - piece.astype(jnp.float32)
        blk_ref[...] = mm(terms_ref[0], inv_first_ref[...])
        blk_ref[...] += mm(terms_ref[1], inv_first_ref[...])
        blk_ref[...] += mm(terms_ref[2], inv_first_ref[...])
        fold_first(blk_ref, fold_ref.at[0], n, fold_ref.at[1])
        for i, block in enumerate(missing_blocks(valid_ref)):
            table = inv_second_ref[block, :]
            part = mm(table, fold_ref[0]) + mm(table, fold_ref[1])
            for c in range(n // LANES):
                at = rebuilt_at(n, c, i * MB)
                acc_ref[pl.ds(at, MB // SUB)] = part[:, c * LANES : (c + 1) * LANES].reshape(MB // SUB, SUB, LANES)


def tile_at(n, part, group, row):
    return (part * (n // LANES) + group) * ((n // 2 + PAD) // SUB) + row // SUB


def rebuilt_at(n, group, row):
    return tile_at(n, 2, 0, 0) + (group * (n // 2) + row) // SUB


def load_rows(ref, n, part, r0, rb, first, last):
    pieces = [ref[pl.ds(tile_at(n, part, g, r0), rb // SUB)].reshape(rb, LANES) for g in range(first, last)]
    return jnp.concatenate(pieces, axis=1)


def sum_stages(devices):
    bits = devices.bit_length() - 1
    if devices != 1 << bits:
        raise ValueError("bad count")
    low = (bits - 1) // 2
    sizes = [1, low, bits - 1 - low] if bits else []
    stages, stride = [], 1
    for size in sizes:
        if size > 0:
            stages.append((1 << size, stride))
        stride <<= max(size, 0)
    return stages


def exchange_kernel(stages, lanes, x_ref, out_ref, sum_ref, recv_ref, rs_send, rs_recv, ag_send, ag_recv):
    me = lax.axis_index("filt")
    digits = [lax.rem(me // stride, radix) for radix, stride in stages]

    def peer_of(stage, digit):
        return me + (digit - digits[stage]) * stages[stage][1]

    barrier = pltpu.get_barrier_semaphore()
    count = 0
    for stage, (radix, _) in enumerate(stages):
        for d in range(1, radix):
            pl.semaphore_signal(
                barrier, inc=1, device_id={"filt": peer_of(stage, lax.rem(digits[stage] + d, radix))},
                device_id_type=pl.DeviceIdType.MESH,
            )
            count += 1
    pl.semaphore_wait(barrier, count)

    plans = []
    slot, sem = 0, 0
    for start, total, order in lanes:
        base, size, plan = start, total, []
        for position, stage in enumerate(order):
            radix = stages[stage][0]
            sub = size // radix
            plan.append((position, stage, radix, base, sub, slot, sem))
            base = base + digits[stage] * sub
            size = sub
            slot += (radix - 1) * sub
            sem += radix - 1
        plans.append(plan)

    def scatter(entry):
        position, stage, radix, base, sub, slot, sem = entry
        source = x_ref if position == 0 else sum_ref
        copies = []
        for d in range(1, radix):
            target = lax.rem(digits[stage] + d, radix)
            copies.append(pltpu.make_async_remote_copy(
                src_ref=source.at[pl.ds(base + target * sub, sub)],
                dst_ref=recv_ref.at[pl.ds(slot + (d - 1) * sub, sub)],
                send_sem=rs_send.at[sem + d - 1], recv_sem=rs_recv.at[sem + d - 1],
                device_id={"filt": peer_of(stage, target)}, device_id_type=pl.DeviceIdType.MESH,
            ))
        return copies

    def add_up(entry):
        position, stage, radix, base, sub, slot, sem = entry
        source = x_ref if position == 0 else sum_ref
        own = base + digits[stage] * sub
        result = out_ref if position == len(stages) - 1 else sum_ref
        step = max(w for w in range(1, 17) if sub % w == 0)

        def add(i, carry):
            value = source[pl.ds(own + i * step, step)]
            for d in range(1, radix):
                value = value + recv_ref[pl.ds(slot + (d - 1) * sub + i * step, step)]
            result[pl.ds(own + i * step, step)] = value
            return carry

        lax.fori_loop(0, sub // step, add, 0)

    def gather(entry):
        position, stage, radix, base, sub, slot, sem = entry
        own = pl.ds(base + digits[stage] * sub, sub)
        copies = []
        for d in range(1, radix):
            target = lax.rem(digits[stage] + d, radix)
            copies.append(pltpu.make_async_remote_copy(
                src_ref=out_ref.at[own], dst_ref=out_ref.at[own],
                send_sem=ag_send.at[sem + d - 1], recv_sem=ag_recv.at[sem + d - 1],
                device_id={"filt": peer_of(stage, target)}, device_id_type=pl.DeviceIdType.MESH,
            ))
        return copies

    depth = len(stages)
    flight = [None] * len(lanes)
    for step in range(2 * depth + 1):
        for lane in range(len(lanes)):
            if flight[lane] is not None:
                for copy in flight[lane]:
                    copy.wait()
                if step <= depth:
                    add_up(plans[lane][step - 1])
            if step < 2 * depth:
                entry = plans[lane][step if step < depth else 2 * depth - 1 - step]
                flight[lane] = scatter(entry) if step < depth else gather(entry)
                for copy in flight[lane]:
                    copy.start()


def fold_first(blk_ref, q_ref, n, rest_ref=None):
    half = n // 2
    hr = half + PAD
    rb = 16
    for r0 in range(0, half, rb):
        rows, srows = pl.ds(r0, rb), pl.ds(hr + r0, rb)
        q_re = blk_ref[rows, :n] - blk_ref[srows, n:]
        q_im = blk_ref[rows, n:] + blk_ref[srows, :n]
        if r0 == 0:
            last = blk_ref[half : half + 8, :n] - blk_ref[hr + half : hr + half + 8, n:]
            row0 = lax.broadcasted_iota(jnp.int32, (rb, n), 0) == 0
            q_im = jnp.where(row0, jnp.broadcast_to(last[0:1], (rb, n)), q_im)
        for at, q in ((rows, q_re), (pl.ds(half + r0, rb), q_im)):
            hi = q.astype(jnp.bfloat16)
            q_ref[at, :] = hi
            if rest_ref is not None:
                rest_ref[at, :] = (q - hi.astype(jnp.float32)).astype(jnp.bfloat16)


def update_kernel(
    n, valid_ref, sums_ref, up_rows_ref, up_cols_ref, survey_ref, b_ref, dual_ref, td_ref, first_ref, second_ref, inv_first_ref,
    inv_second_ref, left_ref, crop_ref, crop_rows_ref,
    codes_ref, duals_ref, raw_ref,
    s_ref, r_ref, dj_ref, xj_ref, ej_ref, blkj_ref, qj_ref,
):
    d_ref, x_ref, q_ref = dj_ref.at[0], xj_ref.at[0], qj_ref.at[0]
    half = n // 2
    hr = half + PAD
    rb = 16
    dict_weight = dict_scale * float(n * n)

    @pl.when(pl.program_id(0) == 0)
    def _():
        x_ref[:n, :] = survey_ref[...].astype(jnp.bfloat16)
        for i, block in enumerate(missing_blocks(valid_ref)):
            for c in range(n // LANES):
                tiles = sums_ref[pl.ds(rebuilt_at(n, c, i * MB), MB // SUB)]
                x_ref[block, c * LANES : (c + 1) * LANES] = tiles.reshape(MB, LANES).astype(jnp.bfloat16)
        q_ref[...] = mm(x_ref[:n, :], first_ref[...]).astype(jnp.bfloat16)
        d_ref[...] = mm(second_ref[...], q_ref[...])
        samples = jnp.concatenate([sums_ref[tile_at(n, 0, c, hr - SUB)] for c in range(TAPS // SUB)], axis=0)
        exact = dict(precision=lax.Precision.HIGHEST, preferred_element_type=jnp.float32)
        r_ref[0] = jnp.dot(jnp.dot(up_rows_ref[...], samples, **exact), up_cols_ref[...], **exact)
        for r0 in range(0, hr, rb):
            rows = pl.ds(r0, rb)
            halves = spectrum_rows(d_ref, hr, half, r0, rb)
            for h in range(2):
                cols = slice(h * half, (h + 1) * half)
                s_re, s_im = halves[h]
                scale = 1.0 / (penalty + jnp.maximum(r_ref[0, rows, cols], 0.0))
                g0, g1 = h * (half // LANES), (h + 1) * (half // LANES)
                s_ref[0, rows, cols] = s_re
                s_ref[1, rows, cols] = s_im
                r_ref[0, rows, cols] = (s_re - load_rows(sums_ref, n, 0, r0, rb, g0, g1)) * scale
                r_ref[1, rows, cols] = (s_im - load_rows(sums_ref, n, 1, r0, rb, g0, g1)) * scale

    per = dual_ref.shape[0]

    def quotients(j):
        dj_ref[j] = mm(left_ref[...], td_ref[j])
        for r0 in range(0, hr, rb):
            rows, srows = pl.ds(r0, rb), pl.ds(hr + r0, rb)
            for h in range(2):
                cols = slice(h * half, (h + 1) * half)
                d_re, d_im = dj_ref[j, rows, cols], dj_ref[j, srows, cols]
                r_re, r_im = r_ref[0, rows, cols], r_ref[1, rows, cols]
                s_re, s_im = s_ref[0, rows, cols], s_ref[1, rows, cols]
                x_re = b_ref[j, 0, rows, cols] + (d_re * r_re + d_im * r_im)
                x_im = b_ref[j, 1, rows, cols] + (d_re * r_im - d_im * r_re)
                xj_ref[j, rows, cols] = x_re.astype(jnp.bfloat16)
                xj_ref[j, srows, cols] = x_im.astype(jnp.bfloat16)
                den = dict_weight + x_re * x_re + x_im * x_im
                inv = pl.reciprocal(den, approx=True)
                inv = inv * (2.0 - den * inv)
                e_re = (x_re * s_re + x_im * s_im + dict_weight * d_re) * inv
                e_im = (x_re * s_im - x_im * s_re + dict_weight * d_im) * inv
                for part, e in ((0, e_re), (1, e_im)):
                    hi = e.astype(jnp.bfloat16)
                    ej_ref[j, pl.ds(part * hr + r0, rb), cols] = hi
                    ej_ref[j, pl.ds((2 + part) * hr + r0, rb), cols] = (e - hi.astype(jnp.float32)).astype(jnp.bfloat16)

    def first_sections(j):
        blkj_ref[j] = mm(xj_ref[j], inv_first_ref[...])
        v = mm(ej_ref[j, : 2 * hr, :], crop_ref[...]) + mm(ej_ref[j, 2 * hr :, :], crop_ref[...])
        v_hi = v.astype(jnp.bfloat16)
        v_lo = (v - v_hi.astype(jnp.float32)).astype(jnp.bfloat16)
        raw_ref[j] = mm(crop_rows_ref[...], v_hi) + mm(crop_rows_ref[...], v_lo)

    def finish(j):
        fold_first(blkj_ref.at[j], qj_ref.at[j], n)
        shifted = mm(inv_second_ref[...], qj_ref[j]) + dual_ref[j].astype(jnp.float32)
        shrunk = shifted - jnp.clip(shifted, -shrink_level, shrink_level)
        codes_ref[j] = shrunk.astype(jnp.bfloat16)
        duals_ref[j] = (shifted - shrunk).astype(jnp.bfloat16)

    quotients(0)
    for j in range(per):
        first_sections(j)
        if j + 1 < per:
            quotients(j + 1)
        finish(j)


def whole_spec(shape):
    return pl.BlockSpec(shape, lambda k: (0,) * len(shape))


def per_filter(per, shape):
    return pl.BlockSpec((per,) + shape, lambda k: (k,) + (0,) * len(shape))


def filters_per_step(count, most):
    return max(w for w in range(1, most + 1) if count % w == 0)


def filter_terms(filters, top, n):
    count = filters.shape[0]
    kernels = filters.reshape(count, FS, FS)
    t = jnp.einsum("kab,bg->kag", kernels, top, precision=lax.Precision.HIGHEST, preferred_element_type=jnp.float32)
    gap = ((0, 0), (0, PAD - FS), (0, 0))
    t = jnp.concatenate([jnp.pad(t[:, :, :n], gap), jnp.pad(t[:, :, n:], gap)], axis=1)
    t0 = t.astype(jnp.bfloat16)
    rest = t - t0.astype(jnp.float32)
    t1 = rest.astype(jnp.bfloat16)
    t2 = (rest - t1.astype(jnp.float32)).astype(jnp.bfloat16)
    return jnp.concatenate([t0, t1, t0, t2, t1, t0], axis=1)


def energy_samples(filters, sample):
    spec = jnp.dot(filters, sample, precision=lax.Precision.HIGHEST, preferred_element_type=jnp.float32)
    energy = jnp.sum(spec * spec, axis=0).reshape(2, TAPS, TAPS).sum(axis=0)
    return jnp.pad(energy, ((0, 0), (0, LANES - TAPS))).reshape(TAPS // SUB, SUB, LANES)


def sum_plan(mesh, tiles):
    devices = mesh.shape["filt"]
    stages = sum_stages(devices)
    units = -(-tiles // devices)
    order = list(range(len(stages)))
    if len(stages) == 3 and units >= 4:
        other = max(1, (units * 4) // 17)
        rest = units - other
        sizes = [(rest + 2) // 3, other, (rest + 1) // 3, rest // 3]
        orders = [order, [0, 2, 1], order, order]
    else:
        sizes, orders = [units], [order]
    lanes, start = [], 0
    for size, own in zip(sizes, orders):
        lanes.append((start, size * devices, own))
        start += size * devices
    return stages, lanes, start


def reduce_tiles(acc, stages, lanes):
    if not stages:
        return acc
    room = 0
    for _, size, order in lanes:
        for stage in order:
            radix = stages[stage][0]
            size //= radix
            room += (radix - 1) * size
    sems = len(lanes) * sum(radix - 1 for radix, _ in stages)
    return pl.pallas_call(
        lambda *refs: exchange_kernel(stages, lanes, *refs),
        out_shape=jax.ShapeDtypeStruct(acc.shape, acc.dtype),
        in_specs=[pl.BlockSpec(memory_space=pltpu.VMEM)],
        out_specs=pl.BlockSpec(memory_space=pltpu.VMEM),
        scratch_shapes=[pltpu.VMEM(acc.shape, jnp.float32), pltpu.VMEM((room, SUB, LANES), jnp.float32)] + [pltpu.SemaphoreType.DMA((sems,))] * 4,
        compiler_params=pltpu.CompilerParams(collective_id=0, has_side_effects=True, vmem_limit_bytes=VMEM_LIMIT),
        name="exchange",
    )(acc)


def make_body(mesh):
    def body(code_maps, dual_maps, survey_tile, filters, valid_blocks):
        n = survey_tile.shape[0]
        count = code_maps.shape[0]
        hr = n // 2 + PAD
        t = make_tables(n)
        td = filter_terms(filters, t["top"], n)
        kdim = td.shape[1]
        f32, bf16 = jnp.float32, jnp.bfloat16
        params = pltpu.CompilerParams(vmem_limit_bytes=VMEM_LIMIT, dimension_semantics=("arbitrary",))
        stages, lanes, tiles = sum_plan(mesh, rebuilt_at(n, n // LANES, 0))
        energy = energy_samples(filters, t["sample"])
        per = filters_per_step(count, SUM_FILTERS)
        acc, b = pl.pallas_call(
            lambda *refs: sums_kernel(n, *refs),
            grid=(count // per,),
            in_specs=[pl.BlockSpec(memory_space=pltpu.SMEM), per_filter(per, (n, n)), per_filter(per, (n, n)), per_filter(per, (kdim, n)),
                      whole_spec((TAPS // SUB, SUB, LANES)), whole_spec((n, n)), whole_spec((2 * hr, n)), whole_spec((2 * hr, kdim)),
                      whole_spec((n, 2 * n)), whole_spec((n, n))],
            out_specs=[whole_spec((tiles, SUB, LANES)), per_filter(per, (2, hr, n))],
            out_shape=[jax.ShapeDtypeStruct((tiles, SUB, LANES), f32), jax.ShapeDtypeStruct((count, 2, hr, n), f32)],
            scratch_shapes=[pltpu.VMEM((per, 2, n, n), bf16)] + [pltpu.VMEM((per, 2 * hr, n), f32)] * 3
            + [pltpu.VMEM((2, hr, n), f32), pltpu.VMEM((3, 2 * hr, n), bf16), pltpu.VMEM((2 * hr, 2 * n), f32), pltpu.VMEM((2, n, n), bf16)],
            compiler_params=params,
            name="sums",
        )(valid_blocks, code_maps, dual_maps, td, energy, t["first"], t["second"], t["left6"], t["inv_first"], t["inv_second"])
        sums = reduce_tiles(acc, stages, lanes)
        per = filters_per_step(count, UPDATE_FILTERS)
        new_codes, new_duals, crops = pl.pallas_call(
            lambda *refs: update_kernel(n, *refs),
            grid=(count // per,),
            in_specs=[pl.BlockSpec(memory_space=pltpu.SMEM), whole_spec((tiles, SUB, LANES)), whole_spec((hr, TAPS)), whole_spec((LANES, n)), whole_spec((n, n)), per_filter(per, (2, hr, n)),
                      per_filter(per, (n, n)), per_filter(per, (kdim, n)), whole_spec((n, n)), whole_spec((2 * hr, n)),
                      whole_spec((n, 2 * n)), whole_spec((n, n)), whole_spec((2 * hr, kdim)),
                      whole_spec((n, 128)), whole_spec((4 * PAD, 2 * hr))],
            out_specs=[per_filter(per, (n, n)), per_filter(per, (n, n)), per_filter(per, (4 * PAD, 128))],
            out_shape=[jax.ShapeDtypeStruct((count, n, n), bf16), jax.ShapeDtypeStruct((count, n, n), bf16),
                       jax.ShapeDtypeStruct((count, 4 * PAD, 128), f32)],
            scratch_shapes=[pltpu.VMEM((2, hr, n), f32), pltpu.VMEM((2, hr, n), f32), pltpu.VMEM((per, 2 * hr, n), f32),
                            pltpu.VMEM((per, 2 * hr, n), bf16), pltpu.VMEM((per, 4 * hr, n), bf16),
                            pltpu.VMEM((per, 2 * hr, 2 * n), f32), pltpu.VMEM((per, n, n), bf16)],
            compiler_params=params,
            name="update",
        )(valid_blocks, sums, t["up_rows"], t["up_cols"], survey_tile, b, dual_maps, td, t["first"], t["second"], t["inv_first"],
          t["inv_second"], t["left6"], t["crop"], t["crop_rows"])
        m = crops[:, : 2 * PAD] + crops[:, 2 * PAD :]
        m = m[:, :, : 2 * PAD] + m[:, :, 2 * PAD : 4 * PAD]
        raw = (m[:, :FS, :FS] + m[:, PAD : PAD + FS, PAD : PAD + FS]) / float(n * n)
        rescale = lax.rsqrt(jnp.mean(raw * raw, axis=(1, 2), keepdims=True) + norm_eps)
        return new_codes, new_duals, (raw * rescale).reshape(count, FS * FS)

    return body


def solution(mesh):
    return jax.shard_map(
        make_body(mesh),
        mesh=mesh,
        in_specs=(
            P("filt", "grp", None),
            P("filt", "grp", None),
            P("grp", None),
            P("filt", "grp"),
            P("grp"),
        ),
        out_specs=(P("filt", "grp", None), P("filt", "grp", None), P("filt", "grp")),
        check_vma=False,
    )
```
